256 devices in a mesh: section: 16 (over x_lo, z), tp: 4 (over x_hi, core), dp: 4 (over y).
Axes of the slice: x: 4 (x_hi: 2, x_lo: 2; x = x_hi * 2 + x_lo), y: 4, z: 8, core: 2. Of those that a mesh axis runs over, the one named last changes fastest.
Arguments:
- memory: bfloat16 [512, 4, 4096], P(None, 'dp', ('section', 'tp')), may hold values from -6 to 6
- queries: bfloat16 [16, 4, 512, 2048], P('section', 'dp', None, 'tp'), may hold values from -6 to 6
- out_grad: bfloat16 [16, 4, 512, 2048], P('section', 'dp', None, 'tp'), may hold values from -6 to 6
- memory_weight: bfloat16 [16, 4096, 2, 2048], P('section', None, None, 'tp'), may hold values from -0.09375 to 0.09375
- lengths: int32 [4], P('dp'), may hold values from 256 to 512
Outputs:
- memory_grad: bfloat16 [512, 4, 4096], P(None, 'dp', ('section', 'tp'))
- query_grad: bfloat16 [16, 4, 512, 2048], P('section', 'dp', None, 'tp')
- weight_grad: bfloat16 [16, 4096, 2, 2048], P('section', 'dp', None, 'tp')
The draws below stay inside these ranges and needn't reach their ends.
Inputs may be any that keep to these rules, and one draw needn't show every extreme that they name: `lengths`: memory positions at or beyond a sequence's length are padding.
All inputs are finite; a program needn't handle non-finite values.
Results may differ from the reference program's by a relative error of at most 0.025.
Values may be sent and summed in bfloat16 or wider, within the bound.
No kernel may reach another device: no remote copies, remote signals or barrier semaphores. Data moves between devices by JAX's collectives and lax.ppermute only.
A program may use at most 128 MiB of HBM per device.

```python
import math
import jax
import jax.numpy as jnp
from jax import lax

D = 4096
HD = 64
S_ENC = 512
T_DEC = 512
SEQ_DEV = 1
SEQS = 4
LAYERS = 16
HC = 2048
N_DP = 4


def touch_ends(array, own_key, least, largest):
    dims = array.shape
    index_at = [jax.random.randint(jax.random.fold_in(own_key, axis), (), 0, dims[axis]) for axis in range(len(dims))]
    array = array.at[tuple(index_at)].set(least)
    longest = dims.index(max(dims))
    index_at[longest] = (index_at[longest] + 1) % dims[longest]
    return array.at[tuple(index_at)].set(largest)


def level_of(own_key, dims, pieces, smallest, top_value):
    level = 1.0
    for axis_at, blocks in pieces:
        heights = jax.random.uniform(jax.random.fold_in(jax.random.fold_in(own_key, 6), axis_at), (blocks,), jnp.float32, smallest / len(pieces), top_value / len(pieces))
        level = level * jnp.repeat(jnp.exp(heights), dims[axis_at] // blocks).reshape((-1,) + (1,) * (len(dims) - 1 - axis_at))
    return level


def scatter_about(rng, dims, scale, limit, pieces=(), kind=jnp.bfloat16):
    array = jax.random.normal(rng, dims, jnp.float32) * scale
    if len(pieces) > 0:
        array = level_of(rng, dims, pieces, -0.22, 0.18) * array
    return jnp.clip(array, min=-limit, max=limit).astype(kind)


def setup_inputs(seed: int = 0) -> dict:
    arg_keys = jax.random.split(jax.random.key(seed), 6)
    memory = scatter_about(arg_keys[0], (S_ENC, SEQS, D), 1.0, 6.0, ((1, 4), (2, 64)))
    queries = scatter_about(arg_keys[1], (LAYERS, SEQS, T_DEC, HC), 1.0, 6.0, ((0, 16), (1, 4), (3, 4)))
    out_grad = scatter_about(arg_keys[2], (LAYERS, SEQS, T_DEC, HC), 1.0, 6.0, ((0, 16), (1, 4), (3, 4)))
    memory_weight = scatter_about(arg_keys[3], (LAYERS, D, 2, HC), D ** -0.5, 0.09375, ((0, 16), (3, 4)))
    lengths = touch_ends(jax.random.randint(arg_keys[4], (SEQS,), S_ENC // 2, S_ENC + 1), jax.random.fold_in(arg_keys[4], 1), S_ENC // 2, S_ENC).astype(jnp.int32)
    return {"memory": memory, "queries": queries, "out_grad": out_grad, "memory_weight": memory_weight, "lengths": lengths}


def pair_grads(query_pair, key_pair, value_pair, grad_pair, key_mask, factor):
    query_wide = query_pair.astype(jnp.float32)
    key_wide = key_pair.astype(jnp.float32)
    value_wide = value_pair.astype(jnp.float32)
    grad_wide = grad_pair.astype(jnp.float32)
    scores = jnp.einsum('thc,shc->hts', query_wide, key_wide) * factor
    weights = jnp.exp(scores) * key_mask[None, None, :]
    attention = weights / lax.optimization_barrier(jnp.sum(weights, axis=2, keepdims=True))
    attention_back = lax.optimization_barrier(attention.astype(jnp.bfloat16)).astype(jnp.float32)
    outputs = jnp.einsum('hts,shc->thc', attention_back, value_wide)
    prob_grad = jnp.einsum('thc,shc->hts', grad_wide, value_wide)
    row_dot = lax.optimization_barrier(jnp.sum(grad_wide * outputs, axis=2))
    score_grad = attention * (prob_grad - jnp.transpose(row_dot)[:, :, None])
    score_back = lax.optimization_barrier(score_grad.astype(jnp.bfloat16)).astype(jnp.float32)
    query_out = (jnp.einsum('hts,shc->thc', score_back, key_wide) * factor).astype(jnp.bfloat16)
    key_out = (jnp.einsum('hts,thc->shc', score_back, query_wide) * factor).astype(jnp.bfloat16)
    value_out = jnp.einsum('hts,thc->shc', attention_back, grad_wide).astype(jnp.bfloat16)
    return (query_out, key_out, value_out)

def attend(query_rows, key_rows, value_rows, grad_rows, key_mask):
    pairs = query_rows.shape[1] // (2 * HD)
    factor = 1.0 / math.sqrt(HD)

    def split(block):
        return block.reshape(block.shape[0], pairs, 2, HD).transpose(1, 0, 2, 3)

    def merge_back(block):
        return block.transpose(1, 0, 2, 3).reshape(block.shape[1], pairs * 2 * HD)
    results = lax.map(lambda items: pair_grads(items[0], items[1], items[2], items[3], key_mask, factor), (split(query_rows), split(key_rows), split(value_rows), split(grad_rows)))
    return (merge_back(results[0]), merge_back(results[1]), merge_back(results[2]))

def reference(memory, queries, out_grad, memory_weight, lengths):
    positions = jnp.arange(S_ENC, dtype=jnp.int32)
    key_masks = (positions[None, :] < lengths[:, None]).astype(jnp.float32)
    memory_wide = memory.astype(jnp.float32)
    grouped = memory_wide.reshape(S_ENC, N_DP, SEQ_DEV, D)

    def one_layer(running, inputs):
        query_layer, grad_layer, weight_layer = inputs
        weight_wide = weight_layer.astype(jnp.float32)
        projected = jnp.einsum('snd,dkc->ksnc', memory_wide, weight_wide).astype(jnp.bfloat16)
        key_seq = jnp.swapaxes(projected[0], 0, 1)
        value_seq = jnp.swapaxes(projected[1], 0, 1)
        query_grad, key_grad, value_grad = lax.map(lambda items: attend(items[0], items[1], items[2], items[3], items[4]), (query_layer, key_seq, value_seq, grad_layer, key_masks))
        grads_wide = jnp.stack([key_grad, value_grad]).transpose(0, 2, 1, 3).astype(jnp.float32)
        running = running + jnp.einsum('ksnc,dkc->snd', grads_wide, weight_wide)
        partial_sums = jnp.einsum('sgnd,ksgnc->gdkc', grouped, grads_wide.reshape(2, S_ENC, N_DP, SEQ_DEV, grads_wide.shape[3]))
        rounded = lax.optimization_barrier(partial_sums.astype(jnp.bfloat16)).astype(jnp.float32)
        weight_grad = lax.optimization_barrier(jnp.sum(rounded, axis=0)).astype(jnp.bfloat16)
        return (running, (query_grad, weight_grad))
    running, outs_layers = lax.scan(one_layer, jnp.zeros((S_ENC, SEQS, D), jnp.float32), (queries, out_grad, memory_weight))
    return (running.astype(jnp.bfloat16), outs_layers[0], outs_layers[1])
```

```python
import functools

import jax
import jax.numpy as jnp
from jax import lax
from jax.experimental import pallas as pl
from jax.experimental.pallas import tpu as pltpu
from jax.sharding import PartitionSpec as P

PLANE = ("section", "tp")
HD = 64
HEADS = 8
F32 = jnp.float32
BF16 = jnp.bfloat16
VMEM = 28 << 20


def index_of(x, z, core):
    x, z = x % 4, z % 8
    return ((x % 2) * 8 + z) * 4 + (x // 2) * 2 + core


def place(i):
    section, tp = divmod(i, 4)
    return (tp // 2) * 2 + section // 8, section % 8, tp % 2


FAR = [
    [index_of(2 * a + px, 2 * b + pz, core) for a in range(2) for b in range(4)]
    for px in range(2)
    for pz in range(2)
    for core in range(2)
]


def beside(value, core):
    return ((value - core) ^ 1) + core


def moves(dx, dz, dcore):
    pairs = []
    for i in range(64):
        x, z, core = place(i)
        pairs.append((i, index_of(beside(x, core) if dx else x, beside(z, core) if dz else z, core ^ dcore)))
    return pairs


NEAR = {(dx, dz): moves(dx, dz, 0) for dx, dz in ((0, 1), (1, 0), (1, 1))}
SWAP = moves(0, 0, 1)


def spread(block, groups):
    count = len(groups[0])
    copies = jnp.broadcast_to(block[None], (count,) + block.shape)
    return lax.all_to_all(copies, PLANE, 0, 0, axis_index_groups=groups)


def collect(blocks, groups):
    parts = lax.all_to_all(blocks, PLANE, 0, 0, axis_index_groups=groups)
    return jnp.sum(parts.astype(F32), axis=0).astype(BF16)


def along_dp(block, step):
    return lax.ppermute(block, "dp", [(d, (d + step) % 4) for d in range(4)])


def swap(block):
    return lax.ppermute(block, PLANE, SWAP)


def near(block, dx, dz):
    return lax.ppermute(block, PLANE, NEAR[dx, dz])


def dot(a, b, dims):
    return lax.dot_general(a, b, (dims, ((), ())), preferred_element_type=F32)


NN = ((1,), (0,))
NT = ((1,), (1,))
TN = ((0,), (0,))


def split_kernel(at_ref, weight_ref, out_ref):
    weight = weight_ref[...].reshape(4, 2, 64, 2, 512)
    weight = jnp.swapaxes(weight, 0, 1).reshape(512, 2, 512)
    out_ref[...] = jnp.swapaxes(weight, 0, 1).reshape(1, 1, 2, 512, 512)


def split_weights(at, weight):
    view = weight.reshape(2, 4, 2, 2, 2, 64, 2, 512)
    return pl.pallas_call(
        split_kernel,
        grid_spec=pltpu.PrefetchScalarGridSpec(
            num_scalar_prefetch=1,
            grid=(4, 2),
            in_specs=[
                pl.BlockSpec(
                    (1, 4, 1, 2, 1, 64, 2, 512),
                    lambda r, h, at: (at[0] ^ (r // 2), 0, at[1] ^ (r % 2), 0, at[2] ^ h, 0, 0, 0),
                )
            ],
            out_specs=pl.BlockSpec((1, 1, 2, 512, 512), lambda r, h, at: (r, h, 0, 0, 0)),
        ),
        out_shape=jax.ShapeDtypeStruct((4, 2, 2, 512, 512), BF16),
        compiler_params=pltpu.CompilerParams(vmem_limit_bytes=VMEM),
        cost_estimate=pl.CostEstimate(flops=0, bytes_accessed=32 << 20, transcendentals=0),
        name="split_weights",
    )(at, view)


def project_kernel(first, count, *refs):
    sums_ref = None if first else refs[0]
    rows_refs = refs[0 if first else 1 :][: 2 * count]
    weight_ref, out_ref, turned = refs[-3:]

    @pl.when(pl.program_id(0) == 0)
    def _():
        for i, rows in enumerate(rows_refs):
            turned[:, i * 512 : (i + 1) * 512] = rows[...].T

    weight = weight_ref[...].reshape(count * 1024, 256)
    total = dot(turned[...], weight, NN)
    if not first:
        total += sums_ref[0]
    out_ref[0] = total.astype(out_ref.dtype)


def project(sums, rows, split, piece, last):
    first, count = sums is None, len(rows) // 2
    columns = pl.BlockSpec((1, 512, 256), lambda i: (i // 2, 0, i % 2))
    return pl.pallas_call(
        functools.partial(project_kernel, first, count),
        grid=(4,),
        in_specs=([] if first else [columns])
        + [pl.BlockSpec((512, 512), lambda i: (0, 0))] * (2 * count)
        + [pl.BlockSpec((count, 2, 1, 512, 256), lambda i: (piece // count, 0, i // 2, 0, i % 2))],
        out_specs=columns,
        scratch_shapes=[pltpu.VMEM((512, 1024 * count), BF16)],
        out_shape=jax.ShapeDtypeStruct((2, 512, 512), BF16 if last else F32),
        compiler_params=pltpu.CompilerParams(vmem_limit_bytes=VMEM),
        cost_estimate=pl.CostEstimate(
            flops=2 * 512 * 1024 * 1024 * count, bytes_accessed=(3 * count + 4) << 20, transcendentals=0
        ),
        name="project",
    )(*([] if first else [sums]), *rows, split)


def attend_kernel(length_ref, query_ref, grad_ref, pair_ref, query_out, grads_out, turned_out):
    position = lax.broadcasted_iota(jnp.int32, (512, 1), 0)
    mask = jnp.where(position < length_ref[0], 1.0, 0.0)
    queries, keys, values = [], [], []
    for head in range(2):
        cols = slice(head * HD, (head + 1) * HD)
        query = query_ref[:, cols] * BF16(0.125)
        grad = grad_ref[:, cols]
        key = pair_ref[0, :, cols]
        value = pair_ref[1, :, cols]
        weights = jnp.exp(dot(key, query, NT)) * mask
        attention = weights * (1.0 / jnp.sum(weights, axis=0, keepdims=True))
        low = attention.astype(BF16)
        prob = dot(value, grad, NT)
        row_dot = jnp.sum(low.astype(F32) * prob, axis=0, keepdims=True)
        score = (attention * (prob - row_dot)).astype(BF16)
        queries.append((dot(score, key, TN) * 0.125).astype(BF16))
        keys.append(dot(score, query, NN).astype(BF16))
        values.append(dot(low, grad, NN).astype(BF16))
    query_out[...] = jnp.concatenate(queries, axis=1)
    key_grad = jnp.concatenate(keys, axis=1)
    value_grad = jnp.concatenate(values, axis=1)
    grads_out[0] = key_grad
    grads_out[1] = value_grad
    turned_out[0] = key_grad.T
    turned_out[1] = value_grad.T


def attend(lengths, queries, out_grad, pair):
    block = pl.BlockSpec((512, 128), lambda i, c: (0, i))
    both = pl.BlockSpec((2, 512, 128), lambda i, c: (0, 0, i))
    return pl.pallas_call(
        attend_kernel,
        grid_spec=pltpu.PrefetchScalarGridSpec(
            num_scalar_prefetch=1,
            grid=(4,),
            in_specs=[block, block, both],
            out_specs=[block, both, pl.BlockSpec((2, 128, 512), lambda i, c: (0, i, 0))],
        ),
        out_shape=[
            jax.ShapeDtypeStruct((512, 512), BF16),
            jax.ShapeDtypeStruct((2, 512, 512), BF16),
            jax.ShapeDtypeStruct((2, 512, 512), BF16),
        ],
        compiler_params=pltpu.CompilerParams(vmem_limit_bytes=VMEM),
        cost_estimate=pl.CostEstimate(flops=8 * 6 * 2 * 512 * 512 * 64 * 4, bytes_accessed=5 << 20, transcendentals=8 << 18),
        name="attend",
    )(lengths, queries, out_grad, pair)


def memory_kernel(weight_ref, turned_ref, *refs):
    total = dot(weight_ref[0, 0, 0], turned_ref[0], NN) + dot(weight_ref[0, 0, 1], turned_ref[1], NN)
    if len(refs) == 2:
        total = total + refs[0][0].astype(F32)
    refs[-1][0] = total.astype(BF16)


def memory_pieces(split, turned, upper, half, sent=None):
    rows = pl.BlockSpec((1, 512, 512), lambda i: (i, 0, 0))
    return pl.pallas_call(
        memory_kernel,
        grid=(2,),
        in_specs=[
            pl.BlockSpec((1, 1, 2, 512, 512), lambda i: (upper - i, half, 0, 0, 0)),
            pl.BlockSpec((2, 512, 512), lambda i: (0, 0, 0)),
        ]
        + ([] if sent is None else [rows]),
        out_specs=rows,
        out_shape=jax.ShapeDtypeStruct((2, 512, 512), BF16),
        compiler_params=pltpu.CompilerParams(vmem_limit_bytes=VMEM),
        cost_estimate=pl.CostEstimate(flops=512 * 2048 * 1024, bytes_accessed=6 << 20, transcendentals=0),
        name="memory_pieces",
    )(split, turned, *([] if sent is None else [sent]))


def weight_kernel(at_ref, mine, other, left, right, across, swapped, g0, g1, g2, gk, gv, out_ref):
    own = pl.program_id(0) < 2
    rows = [jnp.where(own, mine[0], other[0])]
    for i, block in enumerate((left, right, across)):
        rows.append(jnp.where(own, block[0], swapped[i, 0]))
    keys = (g0[0], g1[0], g2[0], gk[...])
    values = (g0[1], g1[1], g2[1], gv[...])
    for_key = sum(dot(a, b, NN) for a, b in zip(rows, keys))
    for_value = sum(dot(a, b, NN) for a, b in zip(rows, values))
    both = jnp.stack([for_key.astype(BF16), for_value.astype(BF16)], axis=0)
    both = jnp.swapaxes(both, 0, 1).reshape(2, 2, 64, 2, 512)
    out_ref[...] = jnp.swapaxes(both, 0, 1).reshape(2, 1, 2, 1, 64, 2, 512)


def weight_rows(at, mine, other, left, right, across, swapped, g0, g1, g2, gk, gv):
    def whole(shape):
        return pl.BlockSpec(shape, lambda i, at: (0,) * len(shape))

    half = pl.BlockSpec((1, 256, 512), lambda i, at: (i % 2, 0, 0))
    out = pl.pallas_call(
        weight_kernel,
        grid_spec=pltpu.PrefetchScalarGridSpec(
            num_scalar_prefetch=1,
            grid=(4,),
            in_specs=[half] * 5
            + [
                pl.BlockSpec((3, 1, 256, 512), lambda i, at: (0, i % 2, 0, 0)),
                whole((2, 512, 512)),
                whole((2, 512, 512)),
                whole((2, 512, 512)),
                whole((512, 512)),
                whole((512, 512)),
            ],
            out_specs=pl.BlockSpec(
                (2, 1, 2, 1, 64, 2, 512), lambda i, at: (0, at[1] ^ (i % 2), 0, at[2] ^ (i // 2), 0, 0, 0)
            ),
        ),
        out_shape=jax.ShapeDtypeStruct((2, 2, 2, 2, 64, 2, 512), BF16),
        compiler_params=pltpu.CompilerParams(vmem_limit_bytes=VMEM),
        cost_estimate=pl.CostEstimate(flops=2 * 2048 * 1024 * 1024, bytes_accessed=12 << 20, transcendentals=0),
        name="weight_rows",
    )(at, mine, other, left, right, across, swapped, g0, g1, g2, gk, gv)
    return out.reshape(1, 1024, 2, 512)


def body(memory, queries, out_grad, memory_weight, lengths):
    section, tp = lax.axis_index("section"), lax.axis_index("tp")
    dp = lax.axis_index("dp").astype(jnp.int32)
    at = jnp.stack([section // 8, section % 2, tp % 2]).astype(jnp.int32)

    split = split_weights(at, memory_weight[0])
    own = spread(memory[:, 0, :].T, FAR).reshape(512, 512)
    own, split = lax.optimization_barrier((own, split))
    mine = [own, near(own, 0, 1), near(own, 1, 0), near(own, 1, 1)]
    other = [swap(piece) for piece in mine]
    sums = project(None, [mine[0], other[0]], split, 0, False)
    sums = project(sums, [mine[1], other[1]], split, 1, False)
    pair = project(sums, [mine[2], other[2], mine[3], other[3]], split, 2, True)

    def block_of(pieces, d):
        moved = (d // 2) ^ at[0]
        rows = []
        for dz in range(2):
            piece = jnp.where(moved == 0, pieces[dz], pieces[2 + dz]).reshape(2, 2, 128, 512)
            rows.append(lax.dynamic_slice(piece, (0, d % 2, 0, 0), (2, 1, 128, 512)).reshape(256, 512))
        return jnp.stack(rows)

    arrived = [along_dp(block_of(mine, (dp + step) % 4), step) for step in (1, 3, 2)]

    query_grad, grads, turned = attend(lengths, queries[0, 0], out_grad[0, 0], pair)
    grads, turned, arrived = lax.optimization_barrier((grads, turned, arrived))

    from_left = along_dp(grads, 1)
    from_right = along_dp(grads, 3)
    across_key = along_dp(from_left[0], 1)
    across_value = along_dp(from_right[1], 3)

    sent_far = swap(memory_pieces(split, turned, 3, 1))
    sent_near = swap(memory_pieces(split, turned, 1, 1))
    far = memory_pieces(split, turned, 3, 0, sent_far)
    from_diagonal, from_x = near(far[0], 1, 1), near(far[1], 1, 0)
    close = memory_pieces(split, turned, 1, 0, sent_near)
    from_z = near(close[0], 0, 1)
    terms = (close[1], from_z, from_x, from_diagonal)
    quarter = sum(term.astype(F32) for term in terms).astype(BF16)
    memory_grad = collect(quarter.reshape(8, 64, 512), FAR).T[:, None, :]

    swapped = swap(jnp.stack(arrived))
    weight_grad = weight_rows(
        at,
        block_of(mine, dp),
        block_of(other, dp),
        *arrived,
        swapped,
        grads,
        from_left,
        from_right,
        across_key,
        across_value,
    )
    return memory_grad, query_grad[None, None], weight_grad


def solution(mesh):
    return jax.shard_map(
        body,
        mesh=mesh,
        in_specs=(
            P(None, "dp", ("section", "tp")),
            P("section", "dp", None, "tp"),
            P("section", "dp", None, "tp"),
            P("section", None, None, "tp"),
            P("dp"),
        ),
        out_specs=(
            P(None, "dp", ("section", "tp")),
            P("section", "dp", None, "tp"),
            P("section", "dp", None, "tp"),
        ),
        check_vma=False,
    )
```

```python
import functools

import jax
import jax.numpy as jnp
from jax import lax
from jax.experimental import pallas as pl
from jax.experimental.pallas import tpu as pltpu
from jax.sharding import PartitionSpec as P

PLANE = ("section", "tp")
HD = 64
HEADS = 8
F32 = jnp.float32
COST = pl.CostEstimate(flops=0, bytes_accessed=1 << 16, transcendentals=0)
BF16 = jnp.bfloat16
VMEM = 28 << 20


def index_of(x, z, core):
    x, z = x % 4, z % 8
    return ((x % 2) * 8 + z) * 4 + (x // 2) * 2 + core


def place(i):
    section, tp = divmod(i, 4)
    return (tp // 2) * 2 + section // 8, section % 8, tp % 2


FAR = [
    [index_of(2 * a + px, 2 * b + pz, core) for a in range(2) for b in range(4)]
    for px in range(2)
    for pz in range(2)
    for core in range(2)
]


def beside(value, core):
    return ((value - core) ^ 1) + core


def moves(dx, dz, dcore):
    pairs = []
    for i in range(64):
        x, z, core = place(i)
        pairs.append((i, index_of(beside(x, core) if dx else x, beside(z, core) if dz else z, core ^ dcore)))
    return pairs


NEAR = {(dx, dz): moves(dx, dz, 0) for dx, dz in ((0, 1), (1, 0), (1, 1))}
SWAP = moves(0, 0, 1)


def spread(block, groups):
    count = len(groups[0])
    copies = jnp.broadcast_to(block[None], (count,) + block.shape)
    return lax.all_to_all(copies, PLANE, 0, 0, axis_index_groups=groups)


def collect(blocks, groups):
    parts = lax.all_to_all(blocks, PLANE, 0, 0, axis_index_groups=groups)
    return jnp.sum(parts.astype(F32), axis=0).astype(BF16)


def along_dp(block, step):
    return lax.ppermute(block, "dp", [(d, (d + step) % 4) for d in range(4)])


def swap(block):
    return lax.ppermute(block, PLANE, SWAP)


def near(block, dx, dz):
    return lax.ppermute(block, PLANE, NEAR[dx, dz])


def dot(a, b, dims):
    return lax.dot_general(a, b, (dims, ((), ())), preferred_element_type=F32)


NN = ((1,), (0,))
NT = ((1,), (1,))
TN = ((0,), (0,))


def split_kernel(at_ref, weight_ref, out_ref):
    weight = weight_ref[...].reshape(4, 2, 64, 2, 512)
    weight = jnp.swapaxes(weight, 0, 1).reshape(512, 2, 512)
    out_ref[...] = jnp.swapaxes(weight, 0, 1).reshape(1, 1, 2, 512, 512)


def split_weights(at, weight):
    view = weight.reshape(2, 4, 2, 2, 2, 64, 2, 512)
    return pl.pallas_call(
        split_kernel,
        grid_spec=pltpu.PrefetchScalarGridSpec(
            num_scalar_prefetch=1,
            grid=(4, 2),
            in_specs=[
                pl.BlockSpec(
                    (1, 4, 1, 2, 1, 64, 2, 512),
                    lambda r, h, at: (at[0] ^ (r // 2), 0, at[1] ^ (r % 2), 0, at[2] ^ h, 0, 0, 0),
                )
            ],
            out_specs=pl.BlockSpec((1, 1, 2, 512, 512), lambda r, h, at: (r, h, 0, 0, 0)),
        ),
        out_shape=jax.ShapeDtypeStruct((4, 2, 2, 512, 512), BF16),
        compiler_params=pltpu.CompilerParams(vmem_limit_bytes=VMEM),
        cost_estimate=COST,
        name="split_weights",
    )(at, view)


def project_kernel(first, count, *refs):
    sums_ref = None if first else refs[0]
    rows_refs = refs[0 if first else 1 :][: 2 * count]
    weight_ref, out_ref, turned = refs[-3:]

    @pl.when(pl.program_id(0) == 0)
    def _():
        for i, rows in enumerate(rows_refs):
            turned[:, i * 512 : (i + 1) * 512] = rows[...].T

    weight = weight_ref[...].reshape(count * 1024, 256)
    total = dot(turned[...], weight, NN)
    if not first:
        total += sums_ref[0]
    out_ref[0] = total.astype(out_ref.dtype)


def project(sums, rows, split, piece, last):
    first, count = sums is None, len(rows) // 2
    columns = pl.BlockSpec((1, 512, 256), lambda i: (i // 2, 0, i % 2))
    return pl.pallas_call(
        functools.partial(project_kernel, first, count),
        grid=(4,),
        in_specs=([] if first else [columns])
        + [pl.BlockSpec((512, 512), lambda i: (0, 0))] * (2 * count)
        + [pl.BlockSpec((count, 2, 1, 512, 256), lambda i: (piece // count, 0, i // 2, 0, i % 2))],
        out_specs=columns,
        scratch_shapes=[pltpu.VMEM((512, 1024 * count), BF16)],
        out_shape=jax.ShapeDtypeStruct((2, 512, 512), BF16 if last else F32),
        compiler_params=pltpu.CompilerParams(vmem_limit_bytes=VMEM),
        cost_estimate=COST,
        name="project",
    )(*([] if first else [sums]), *rows, split)


def attend_kernel(length_ref, query_ref, grad_ref, pair_ref, query_out, grads_out, turned_out):
    position = lax.broadcasted_iota(jnp.int32, (512, 1), 0)
    mask = jnp.where(position < length_ref[0], 1.0, 0.0)
    queries, keys, values = [], [], []
    for head in range(2):
        cols = slice(head * HD, (head + 1) * HD)
        query = query_ref[:, cols] * BF16(0.125)
        grad = grad_ref[:, cols]
        key = pair_ref[0, :, cols]
        value = pair_ref[1, :, cols]
        weights = jnp.exp(dot(key, query, NT)) * mask
        attention = weights * (1.0 / jnp.sum(weights, axis=0, keepdims=True))
        low = attention.astype(BF16)
        prob = dot(value, grad, NT)
        row_dot = jnp.sum(low.astype(F32) * prob, axis=0, keepdims=True)
        score = (attention * (prob - row_dot)).astype(BF16)
        queries.append((dot(score, key, TN) * 0.125).astype(BF16))
        keys.append(dot(score, query, NN).astype(BF16))
        values.append(dot(low, grad, NN).astype(BF16))
    query_out[...] = jnp.concatenate(queries, axis=1)
    key_grad = jnp.concatenate(keys, axis=1)
    value_grad = jnp.concatenate(values, axis=1)
    grads_out[0] = key_grad
    grads_out[1] = value_grad
    turned_out[0] = key_grad.T
    turned_out[1] = value_grad.T


def attend(lengths, queries, out_grad, pair):
    block = pl.BlockSpec((512, 128), lambda i, c: (0, i))
    both = pl.BlockSpec((2, 512, 128), lambda i, c: (0, 0, i))
    return pl.pallas_call(
        attend_kernel,
        grid_spec=pltpu.PrefetchScalarGridSpec(
            num_scalar_prefetch=1,
            grid=(4,),
            in_specs=[block, block, both],
            out_specs=[block, both, pl.BlockSpec((2, 128, 512), lambda i, c: (0, i, 0))],
        ),
        out_shape=[
            jax.ShapeDtypeStruct((512, 512), BF16),
            jax.ShapeDtypeStruct((2, 512, 512), BF16),
            jax.ShapeDtypeStruct((2, 512, 512), BF16),
        ],
        compiler_params=pltpu.CompilerParams(vmem_limit_bytes=VMEM),
        cost_estimate=COST,
        name="attend",
    )(lengths, queries, out_grad, pair)


def other_kernel(weight_ref, turned_ref, out_ref):
    total = dot(weight_ref[0, 0, 0], turned_ref[0], NN) + dot(weight_ref[0, 0, 1], turned_ref[1], NN)
    out_ref[0] = total.astype(BF16)


def own_kernel(weight_ref, turned_ref, sent_ref, *outs):
    total = dot(weight_ref[0, 0, 0], turned_ref[0], NN) + dot(weight_ref[0, 0, 1], turned_ref[1], NN)
    total = (total + sent_ref[0].astype(F32)).astype(BF16)
    for i, out_ref in enumerate(outs):

        @pl.when(pl.program_id(0) == i)
        def _():
            out_ref[...] = total


def memory_pieces(split, turned, upper, sent=None):
    rows = pl.BlockSpec((1, 512, 512), lambda i: (i, 0, 0))
    half = 1 if sent is None else 0
    one = jax.ShapeDtypeStruct((512, 512), BF16)
    return pl.pallas_call(
        other_kernel if sent is None else own_kernel,
        grid=(2,),
        in_specs=[
            pl.BlockSpec((1, 1, 2, 512, 512), lambda i: (upper - i, half, 0, 0, 0)),
            pl.BlockSpec((2, 512, 512), lambda i: (0, 0, 0)),
        ]
        + ([] if sent is None else [rows]),
        out_specs=rows if sent is None else [pl.BlockSpec((512, 512), lambda i: (0, 0))] * 2,
        out_shape=jax.ShapeDtypeStruct((2, 512, 512), BF16) if sent is None else [one, one],
        compiler_params=pltpu.CompilerParams(vmem_limit_bytes=VMEM),
        cost_estimate=COST,
        name="memory_pieces",
    )(split, turned, *([] if sent is None else [sent]))


def sum_kernel(at_ref, mine, other, left, right, swapped, g0, g1, g2, out_ref):
    own = pl.program_id(0) < 2
    pairs = ((mine[0], other[0]), (left[0], swapped[0, 0]), (right[0], swapped[1, 0]))
    rows = [jnp.where(own, here, there) for here, there in pairs]
    for kind in range(2):
        out_ref[0, kind] = sum(dot(a, b[kind], NN) for a, b in zip(rows, (g0, g1, g2)))


def last_kernel(at_ref, across, swapped, key, value, sums, out_ref):
    rows = jnp.where(pl.program_id(0) < 2, across[0], swapped[0, 0])
    for_key = sums[0, 0] + dot(rows, key[...], NN)
    for_value = sums[0, 1] + dot(rows, value[...], NN)
    both = jnp.stack([for_key.astype(BF16), for_value.astype(BF16)], axis=0)
    both = jnp.swapaxes(both, 0, 1).reshape(2, 2, 64, 2, 512)
    out_ref[...] = jnp.swapaxes(both, 0, 1).reshape(2, 1, 2, 1, 64, 2, 512)


HALF = pl.BlockSpec((1, 256, 512), lambda i, at: (i % 2, 0, 0))
SUMS = pl.BlockSpec((1, 2, 256, 512), lambda i, at: (i, 0, 0, 0))


def whole(shape):
    return pl.BlockSpec(shape, lambda i, at: (0,) * len(shape))


def weight_sums(at, mine, other, left, right, swapped, grads):
    return pl.pallas_call(
        sum_kernel,
        grid_spec=pltpu.PrefetchScalarGridSpec(
            num_scalar_prefetch=1,
            grid=(4,),
            in_specs=[HALF] * 4
            + [pl.BlockSpec((2, 1, 256, 512), lambda i, at: (0, i % 2, 0, 0))]
            + [whole((2, 512, 512))] * 3,
            out_specs=SUMS,
        ),
        out_shape=jax.ShapeDtypeStruct((4, 2, 256, 512), F32),
        compiler_params=pltpu.CompilerParams(vmem_limit_bytes=VMEM),
        cost_estimate=COST,
        name="weight_sums",
    )(at, mine, other, left, right, swapped, *grads)


def weight_rows(at, across, swapped, key, value, sums):
    out = pl.pallas_call(
        last_kernel,
        grid_spec=pltpu.PrefetchScalarGridSpec(
            num_scalar_prefetch=1,
            grid=(4,),
            in_specs=[HALF, pl.BlockSpec((1, 1, 256, 512), lambda i, at: (2, i % 2, 0, 0))]
            + [whole((512, 512)), whole((512, 512)), SUMS],
            out_specs=pl.BlockSpec(
                (2, 1, 2, 1, 64, 2, 512), lambda i, at: (0, at[1] ^ (i % 2), 0, at[2] ^ (i // 2), 0, 0, 0)
            ),
        ),
        out_shape=jax.ShapeDtypeStruct((2, 2, 2, 2, 64, 2, 512), BF16),
        compiler_params=pltpu.CompilerParams(vmem_limit_bytes=VMEM),
        cost_estimate=COST,
        name="weight_rows",
    )(at, across, swapped, key, value, sums)
    return out.reshape(1, 1024, 2, 512)


def body(memory, queries, out_grad, memory_weight, lengths):
    section, tp = lax.axis_index("section"), lax.axis_index("tp")
    dp = lax.axis_index("dp").astype(jnp.int32)
    at = jnp.stack([section // 8, section % 2, tp % 2]).astype(jnp.int32)

    split = split_weights(at, memory_weight[0])
    own = spread(memory[:, 0, :].T, FAR).reshape(512, 512)
    own, split = lax.optimization_barrier((own, split))
    own_other = swap(own)
    from_z, from_x, from_diagonal = near(own, 0, 1), near(own, 1, 0), near(own, 1, 1)
    sums = project(None, [own, own_other], split, 0, False)
    sums, from_z, from_x, from_diagonal = lax.optimization_barrier((sums, from_z, from_x, from_diagonal))
    mine = [own, from_z, from_x, from_diagonal]
    other = [own_other] + [swap(piece) for piece in mine[1:]]
    sums = project(sums, [mine[1], other[1]], split, 1, False)
    pair = project(sums, [mine[2], other[2], mine[3], other[3]], split, 2, True)

    def block_of(pieces, d):
        moved = (d // 2) ^ at[0]
        rows = []
        for dz in range(2):
            piece = jnp.where(moved == 0, pieces[dz], pieces[2 + dz]).reshape(2, 2, 128, 512)
            rows.append(lax.dynamic_slice(piece, (0, d % 2, 0, 0), (2, 1, 128, 512)).reshape(256, 512))
        return jnp.stack(rows)

    arrived = [along_dp(block_of(mine, (dp + step) % 4), step) for step in (1, 3, 2)]

    query_grad, grads, turned = attend(lengths, queries[0, 0], out_grad[0, 0], pair)
    left, right, across = arrived
    grads, turned, left, right = lax.optimization_barrier((grads, turned, left, right))

    from_left = along_dp(grads, 1)
    from_right = along_dp(grads, 3)
    for_other, across = lax.optimization_barrier((memory_pieces(split, turned, 3), across))
    sent_far = swap(for_other)
    sent_near = swap(memory_pieces(split, turned, 1))
    diagonal, far_x = memory_pieces(split, turned, 3, sent_far)
    from_diagonal, from_x = near(diagonal, 1, 1), near(far_x, 1, 0)
    close_z, close = memory_pieces(split, turned, 1, sent_near)
    from_z = near(close_z, 0, 1)
    terms = (close, from_z, from_x, from_diagonal)
    quarter = sum(term.astype(F32) for term in terms).astype(BF16)
    _, from_left, from_right = lax.optimization_barrier((quarter, from_left, from_right))
    across_key = along_dp(from_left[0], 1)
    across_value = along_dp(from_right[1], 3)
    memory_grad = collect(quarter.reshape(8, 64, 512), FAR).T[:, None, :]

    swapped = swap(jnp.stack([left, right, across]))
    rows, rows_other = block_of(mine, dp), block_of(other, dp)
    sums = weight_sums(at, rows, rows_other, left, right, swapped, (grads, from_left, from_right))
    sums, across_key, across_value = lax.optimization_barrier((sums, across_key, across_value))
    weight_grad = weight_rows(at, across, swapped, across_key, across_value, sums)
    return memory_grad, query_grad[None, None], weight_grad


def solution(mesh):
    return jax.shard_map(
        body,
        mesh=mesh,
        in_specs=(
            P(None, "dp", ("section", "tp")),
            P("section", "dp", None, "tp"),
            P("section", "dp", None, "tp"),
            P("section", None, None, "tp"),
            P("dp"),
        ),
        out_specs=(
            P(None, "dp", ("section", "tp")),
            P("section", "dp", None, "tp"),
            P("section", "dp", None, "tp"),
        ),
        check_vma=False,
    )
```

```python
import functools

import jax
import jax.numpy as jnp
from jax import lax
from jax.experimental import pallas as pl
from jax.experimental.pallas import tpu as pltpu
from jax.sharding import PartitionSpec as P

PLANE = ("section", "tp")
HD = 64
HEADS = 8
F32 = jnp.float32
COST = pl.CostEstimate(flops=0, bytes_accessed=1 << 16, transcendentals=0)
BF16 = jnp.bfloat16
VMEM = 28 << 20


def index_of(x, z, core):
    x, z = x % 4, z % 8
    return ((x % 2) * 8 + z) * 4 + (x // 2) * 2 + core


def place(i):
    section, tp = divmod(i, 4)
    return (tp // 2) * 2 + section // 8, section % 8, tp % 2


FAR = [
    [index_of(2 * a + px, 2 * b + pz, core) for a in range(2) for b in range(4)]
    for px in range(2)
    for pz in range(2)
    for core in range(2)
]


def beside(value, core):
    return ((value - core) ^ 1) + core


def moves(dx, dz, dcore):
    pairs = []
    for i in range(64):
        x, z, core = place(i)
        pairs.append((i, index_of(beside(x, core) if dx else x, beside(z, core) if dz else z, core ^ dcore)))
    return pairs


NEAR = {(dx, dz): moves(dx, dz, 0) for dx, dz in ((0, 1), (1, 0), (1, 1))}
SWAP = moves(0, 0, 1)


def spread(block, groups):
    count = len(groups[0])
    copies = jnp.broadcast_to(block[None], (count,) + block.shape)
    return lax.all_to_all(copies, PLANE, 0, 0, axis_index_groups=groups)


def collect(blocks, groups):
    return lax.all_to_all(blocks, PLANE, 0, 0, axis_index_groups=groups)


def along_dp(block, step):
    pairs = []
    for tp in range(4):
        for d in range(4):
            pairs.append((tp * 4 + d, tp * 4 + (d + (-step if tp % 2 else step)) % 4))
    return lax.ppermute(block, ("tp", "dp"), pairs)


def swap(block):
    return lax.ppermute(block, PLANE, SWAP)


def near(block, dx, dz):
    return lax.ppermute(block, PLANE, NEAR[dx, dz])


def dot(a, b, dims):
    return lax.dot_general(a, b, (dims, ((), ())), preferred_element_type=F32)


NN = ((1,), (0,))
NT = ((1,), (1,))
TN = ((0,), (0,))


def split_kernel(at_ref, weight_ref, out_ref):
    weight = weight_ref[...].reshape(4, 2, 64, 2, 512)
    weight = jnp.swapaxes(weight, 0, 1).reshape(512, 2, 512)
    out_ref[...] = jnp.swapaxes(weight, 0, 1).reshape(1, 1, 2, 512, 512)


def split_weights(at, weight):
    view = weight.reshape(2, 4, 2, 2, 2, 64, 2, 512)
    return pl.pallas_call(
        split_kernel,
        grid_spec=pltpu.PrefetchScalarGridSpec(
            num_scalar_prefetch=1,
            grid=(4, 2),
            in_specs=[
                pl.BlockSpec(
                    (1, 4, 1, 2, 1, 64, 2, 512),
                    lambda r, h, at: (at[0] ^ (r // 2), 0, at[1] ^ (r % 2), 0, at[2] ^ h, 0, 0, 0),
                )
            ],
            out_specs=pl.BlockSpec((1, 1, 2, 512, 512), lambda r, h, at: (r, h, 0, 0, 0)),
        ),
        out_shape=jax.ShapeDtypeStruct((4, 2, 2, 512, 512), BF16),
        compiler_params=pltpu.CompilerParams(vmem_limit_bytes=VMEM),
        cost_estimate=COST,
        name="split_weights",
    )(at, view)


def project_kernel(first, count, *refs):
    sums_ref = None if first else refs[0]
    rows_refs = refs[0 if first else 1 :][: 2 * count]
    weight_ref, out_ref, turned = refs[-3:]

    @pl.when(pl.program_id(0) == 0)
    def _():
        for i, rows in enumerate(rows_refs):
            turned[:, i * 512 : (i + 1) * 512] = rows[...].T

    weight = weight_ref[...].reshape(count * 1024, 256)
    total = dot(turned[...], weight, NN)
    if not first:
        total += sums_ref[0]
    out_ref[0] = total.astype(out_ref.dtype)


def project(sums, rows, split, piece, last):
    first, count = sums is None, len(rows) // 2
    columns = pl.BlockSpec((1, 512, 256), lambda i: (i // 2, 0, i % 2))
    return pl.pallas_call(
        functools.partial(project_kernel, first, count),
        grid=(4,),
        in_specs=([] if first else [columns])
        + [pl.BlockSpec((512, 512), lambda i: (0, 0))] * (2 * count)
        + [pl.BlockSpec((count, 2, 1, 512, 256), lambda i: (piece // count, 0, i // 2, 0, i % 2))],
        out_specs=columns,
        scratch_shapes=[pltpu.VMEM((512, 1024 * count), BF16)],
        out_shape=jax.ShapeDtypeStruct((2, 512, 512), BF16 if last else F32),
        compiler_params=pltpu.CompilerParams(vmem_limit_bytes=VMEM),
        cost_estimate=COST,
        name="project",
    )(*([] if first else [sums]), *rows, split)


def attend_kernel(length_ref, query_ref, grad_ref, pair_ref, query_out, grads_out, turned_out):
    position = lax.broadcasted_iota(jnp.int32, (512, 1), 0)
    mask = jnp.where(position < length_ref[0], 1.0, 0.0)
    queries, keys, values = [], [], []
    for head in range(2):
        cols = slice(head * HD, (head + 1) * HD)
        query = query_ref[:, cols] * BF16(0.125)
        grad = grad_ref[:, cols]
        key = pair_ref[0, :, cols]
        value = pair_ref[1, :, cols]
        weights = jnp.exp(dot(key, query, NT)) * mask
        attention = weights * (1.0 / jnp.sum(weights, axis=0, keepdims=True))
        low = attention.astype(BF16)
        prob = dot(value, grad, NT)
        row_dot = jnp.sum(low.astype(F32) * prob, axis=0, keepdims=True)
        score = (attention * (prob - row_dot)).astype(BF16)
        queries.append((dot(score, key, TN) * 0.125).astype(BF16))
        keys.append(dot(score, query, NN).astype(BF16))
        values.append(dot(low, grad, NN).astype(BF16))
    query_out[...] = jnp.concatenate(queries, axis=1)
    key_grad = jnp.concatenate(keys, axis=1)
    value_grad = jnp.concatenate(values, axis=1)
    grads_out[0] = key_grad
    grads_out[1] = value_grad
    turned_out[0] = key_grad.T
    turned_out[1] = value_grad.T


def attend(lengths, queries, out_grad, pair):
    block = pl.BlockSpec((512, 128), lambda i, c: (0, i))
    both = pl.BlockSpec((2, 512, 128), lambda i, c: (0, 0, i))
    return pl.pallas_call(
        attend_kernel,
        grid_spec=pltpu.PrefetchScalarGridSpec(
            num_scalar_prefetch=1,
            grid=(4,),
            in_specs=[block, block, both],
            out_specs=[block, both, pl.BlockSpec((2, 128, 512), lambda i, c: (0, i, 0))],
        ),
        out_shape=[
            jax.ShapeDtypeStruct((512, 512), BF16),
            jax.ShapeDtypeStruct((2, 512, 512), BF16),
            jax.ShapeDtypeStruct((2, 512, 512), BF16),
        ],
        compiler_params=pltpu.CompilerParams(vmem_limit_bytes=VMEM),
        cost_estimate=COST,
        name="attend",
    )(lengths, queries, out_grad, pair)


def other_kernel(weight_ref, turned_ref, out_ref):
    total = dot(weight_ref[0, 0, 0], turned_ref[0], NN) + dot(weight_ref[0, 0, 1], turned_ref[1], NN)
    out_ref[0] = total.astype(BF16)


def own_kernel(weight_ref, turned_ref, sent_ref, *outs):
    total = dot(weight_ref[0, 0, 0], turned_ref[0], NN) + dot(weight_ref[0, 0, 1], turned_ref[1], NN)
    total = (total + sent_ref[0].astype(F32)).astype(BF16)
    for i, out_ref in enumerate(outs):

        @pl.when(pl.program_id(0) == i)
        def _():
            out_ref[...] = total


def memory_pieces(split, turned, upper, sent=None):
    rows = pl.BlockSpec((1, 512, 512), lambda i: (i, 0, 0))
    half = 1 if sent is None else 0
    one = jax.ShapeDtypeStruct((512, 512), BF16)
    return pl.pallas_call(
        other_kernel if sent is None else own_kernel,
        grid=(2,),
        in_specs=[
            pl.BlockSpec((1, 1, 2, 512, 512), lambda i: (upper - i, half, 0, 0, 0)),
            pl.BlockSpec((2, 512, 512), lambda i: (0, 0, 0)),
        ]
        + ([] if sent is None else [rows]),
        out_specs=rows if sent is None else [pl.BlockSpec((512, 512), lambda i: (0, 0))] * 2,
        out_shape=jax.ShapeDtypeStruct((2, 512, 512), BF16) if sent is None else [one, one],
        compiler_params=pltpu.CompilerParams(vmem_limit_bytes=VMEM),
        cost_estimate=COST,
        name="memory_pieces",
    )(split, turned, *([] if sent is None else [sent]))


def sum_kernel(at_ref, mine, other, behind, ahead, swapped, g0, g1, g2, out_ref):
    own = pl.program_id(0) < 2
    pairs = ((mine[0], other[0]), (behind[0], swapped[1, 0]), (ahead[0], swapped[0, 0]))
    rows = [jnp.where(own, here, there) for here, there in pairs]
    for kind in range(2):
        out_ref[0, kind] = sum(dot(a, b[kind], NN) for a, b in zip(rows, (g0, g1, g2)))


def last_kernel(at_ref, across, swapped, grads, sums, out_ref):
    rows = jnp.where(pl.program_id(0) < 2, across[0], swapped[0, 0])
    for_key = sums[0, 0] + dot(rows, grads[0], NN)
    for_value = sums[0, 1] + dot(rows, grads[1], NN)
    both = jnp.stack([for_key.astype(BF16), for_value.astype(BF16)], axis=0)
    both = jnp.swapaxes(both, 0, 1).reshape(2, 2, 64, 2, 512)
    out_ref[...] = jnp.swapaxes(both, 0, 1).reshape(2, 1, 2, 1, 64, 2, 512)


HALF = pl.BlockSpec((1, 256, 512), lambda i, at: (i % 2, 0, 0))
SUMS = pl.BlockSpec((1, 2, 256, 512), lambda i, at: (i, 0, 0, 0))


def whole(shape):
    return pl.BlockSpec(shape, lambda i, at: (0,) * len(shape))


def weight_sums(at, mine, other, behind, ahead, swapped, grads):
    return pl.pallas_call(
        sum_kernel,
        grid_spec=pltpu.PrefetchScalarGridSpec(
            num_scalar_prefetch=1,
            grid=(4,),
            in_specs=[HALF] * 4
            + [pl.BlockSpec((2, 1, 256, 512), lambda i, at: (0, i % 2, 0, 0))]
            + [whole((2, 512, 512))] * 3,
            out_specs=SUMS,
        ),
        out_shape=jax.ShapeDtypeStruct((4, 2, 256, 512), F32),
        compiler_params=pltpu.CompilerParams(vmem_limit_bytes=VMEM),
        cost_estimate=COST,
        name="weight_sums",
    )(at, mine, other, behind, ahead, swapped, *grads)


def weight_rows(at, across, swapped, grads, sums):
    out = pl.pallas_call(
        last_kernel,
        grid_spec=pltpu.PrefetchScalarGridSpec(
            num_scalar_prefetch=1,
            grid=(4,),
            in_specs=[HALF, pl.BlockSpec((1, 1, 256, 512), lambda i, at: (2, i % 2, 0, 0))]
            + [whole((2, 512, 512)), SUMS],
            out_specs=pl.BlockSpec(
                (2, 1, 2, 1, 64, 2, 512), lambda i, at: (0, at[1] ^ (i % 2), 0, at[2] ^ (i // 2), 0, 0, 0)
            ),
        ),
        out_shape=jax.ShapeDtypeStruct((2, 2, 2, 2, 64, 2, 512), BF16),
        compiler_params=pltpu.CompilerParams(vmem_limit_bytes=VMEM),
        cost_estimate=COST,
        name="weight_rows",
    )(at, across, swapped, grads, sums)
    return out.reshape(1, 1024, 2, 512)


def body(memory, queries, out_grad, memory_weight, lengths):
    section, tp = lax.axis_index("section"), lax.axis_index("tp")
    dp = lax.axis_index("dp").astype(jnp.int32)
    at = jnp.stack([section // 8, section % 2, tp % 2]).astype(jnp.int32)

    split = split_weights(at, memory_weight[0])
    own = spread(memory[:, 0, :].T, FAR).reshape(512, 512)
    own, split = lax.optimization_barrier((own, split))
    own_other = swap(own)
    from_z, from_x, from_diagonal = near(own, 0, 1), near(own, 1, 0), near(own, 1, 1)
    sums = project(None, [own, own_other], split, 0, False)
    sums, from_z, from_x, from_diagonal = lax.optimization_barrier((sums, from_z, from_x, from_diagonal))
    mine = [own, from_z, from_x, from_diagonal]
    other = [own_other] + [swap(piece) for piece in mine[1:]]
    sums = project(sums, [mine[1], other[1]], split, 1, False)
    pair = project(sums, [mine[2], other[2], mine[3], other[3]], split, 2, True)

    def block_of(pieces, d):
        moved = (d // 2) ^ at[0]
        rows = []
        for dz in range(2):
            piece = jnp.where(moved == 0, pieces[dz], pieces[2 + dz]).reshape(2, 2, 128, 512)
            rows.append(lax.dynamic_slice(piece, (0, d % 2, 0, 0), (2, 1, 128, 512)).reshape(256, 512))
        return jnp.stack(rows)

    way = 1 - 2 * at[2]
    arrived = [along_dp(block_of(mine, (dp + 4 + way * step) % 4), step) for step in (1, -1, 2)]

    query_grad, grads, turned = attend(lengths, queries[0, 0], out_grad[0, 0], pair)
    behind, ahead, across = arrived
    grads, turned, behind, ahead = lax.optimization_barrier((grads, turned, behind, ahead))

    from_behind = along_dp(grads, 1)
    from_ahead = along_dp(grads, -1)
    for_other, across = lax.optimization_barrier((memory_pieces(split, turned, 3), across))
    sent_far = swap(for_other)
    sent_near = swap(memory_pieces(split, turned, 1))
    diagonal, far_x = memory_pieces(split, turned, 3, sent_far)
    from_diagonal, from_x = near(diagonal, 1, 1), near(far_x, 1, 0)
    close_z, close = memory_pieces(split, turned, 1, sent_near)
    from_z = near(close_z, 0, 1)
    terms = (close, from_z, from_x, from_diagonal)
    quarter = sum(term.astype(F32) for term in terms).astype(BF16)
    _, from_behind, from_ahead = lax.optimization_barrier((quarter, from_behind, from_ahead))
    from_across = along_dp(from_behind, 1)
    parts = collect(quarter.reshape(8, 64, 512), FAR)

    swapped = swap(jnp.stack([behind, ahead, across]))
    rows, rows_other = block_of(mine, dp), block_of(other, dp)
    sums = weight_sums(at, rows, rows_other, behind, ahead, swapped, (grads, from_behind, from_ahead))
    sums, from_across = lax.optimization_barrier((sums, from_across))
    weight_grad = weight_rows(at, across, swapped, from_across, sums)
    parts, weight_grad = lax.optimization_barrier((parts, weight_grad))
    memory_grad = jnp.sum(parts.astype(F32), axis=0).astype(BF16).T[:, None, :]
    return memory_grad, query_grad[None, None], weight_grad


def solution(mesh):
    return jax.shard_map(
        body,
        mesh=mesh,
        in_specs=(
            P(None, "dp", ("section", "tp")),
            P("section", "dp", None, "tp"),
            P("section", "dp", None, "tp"),
            P("section", None, None, "tp"),
            P("dp"),
        ),
        out_specs=(
            P(None, "dp", ("section", "tp")),
            P("section", "dp", None, "tp"),
            P("section", "dp", None, "tp"),
        ),
        check_vma=False,
    )
```

```python
import functools

import jax
import jax.numpy as jnp
from jax import lax
from jax.experimental import pallas as pl
from jax.experimental.pallas import tpu as pltpu
from jax.sharding import PartitionSpec as P

PLANE = ("section", "tp")
HD = 64
HEADS = 8
F32 = jnp.float32
COST = pl.CostEstimate(flops=0, bytes_accessed=1 << 16, transcendentals=0)
BF16 = jnp.bfloat16
VMEM = 28 << 20


def index_of(x, z, core):
    x, z = x % 4, z % 8
    return ((x % 2) * 8 + z) * 4 + (x // 2) * 2 + core


def place(i):
    section, tp = divmod(i, 4)
    return (tp // 2) * 2 + section // 8, section % 8, tp % 2


FAR = [
    [index_of(2 * a + px, 2 * b + pz, core) for a in range(2) for b in range(4)]
    for px in range(2)
    for pz in range(2)
    for core in range(2)
]


def beside(value, core):
    return ((value - core) ^ 1) + core


def moves(dx, dz, dcore):
    pairs = []
    for i in range(64):
        x, z, core = place(i)
        pairs.append((i, index_of(beside(x, core) if dx else x, beside(z, core) if dz else z, core ^ dcore)))
    return pairs


NEAR = {(dx, dz): moves(dx, dz, 0) for dx, dz in ((0, 1), (1, 0), (1, 1))}
SWAP = moves(0, 0, 1)


def spread(block, groups):
    count = len(groups[0])
    copies = jnp.broadcast_to(block[None], (count,) + block.shape)
    return lax.all_to_all(copies, PLANE, 0, 0, axis_index_groups=groups)


def collect(blocks, groups):
    return lax.all_to_all(blocks, PLANE, 0, 0, axis_index_groups=groups)


def along_dp(block, step):
    pairs = []
    for tp in range(4):
        for d in range(4):
            pairs.append((tp * 4 + d, tp * 4 + (d + (-step if tp % 2 else step)) % 4))
    return lax.ppermute(block, ("tp", "dp"), pairs)


def swap(block):
    return lax.ppermute(block, PLANE, SWAP)


def near(block, dx, dz):
    return lax.ppermute(block, PLANE, NEAR[dx, dz])


def dot(a, b, dims):
    return lax.dot_general(a, b, (dims, ((), ())), preferred_element_type=F32)


NN = ((1,), (0,))
NT = ((1,), (1,))
TN = ((0,), (0,))


def split_kernel(at_ref, weight_ref, out_ref):
    weight = weight_ref[...].reshape(4, 2, 64, 2, 512)
    weight = jnp.swapaxes(weight, 0, 1).reshape(512, 2, 512)
    out_ref[...] = jnp.swapaxes(weight, 0, 1).reshape(1, 1, 2, 512, 512)


def split_weights(at, weight):
    view = weight.reshape(2, 4, 2, 2, 2, 64, 2, 512)
    return pl.pallas_call(
        split_kernel,
        grid_spec=pltpu.PrefetchScalarGridSpec(
            num_scalar_prefetch=1,
            grid=(4, 2),
            in_specs=[
                pl.BlockSpec(
                    (1, 4, 1, 2, 1, 64, 2, 512),
                    lambda r, h, at: (at[0] ^ (r // 2), 0, at[1] ^ (r % 2), 0, at[2] ^ h, 0, 0, 0),
                )
            ],
            out_specs=pl.BlockSpec((1, 1, 2, 512, 512), lambda r, h, at: (r, h, 0, 0, 0)),
        ),
        out_shape=jax.ShapeDtypeStruct((4, 2, 2, 512, 512), BF16),
        compiler_params=pltpu.CompilerParams(vmem_limit_bytes=VMEM),
        cost_estimate=COST,
        name="split_weights",
    )(at, view)


def project_kernel(first, count, *refs):
    sums_ref = None if first else refs[0]
    rows_refs = refs[0 if first else 1 :][: 2 * count]
    weight_ref, out_ref, turned = refs[-3:]

    @pl.when(pl.program_id(0) == 0)
    def _():
        for i, rows in enumerate(rows_refs):
            turned[:, i * 512 : (i + 1) * 512] = rows[...].T

    weight = weight_ref[...].reshape(count * 1024, 256)
    total = dot(turned[...], weight, NN)
    if not first:
        total += sums_ref[0]
    out_ref[0] = total.astype(out_ref.dtype)


def project(sums, rows, split, piece, last):
    first, count = sums is None, len(rows) // 2
    columns = pl.BlockSpec((1, 512, 256), lambda i: (i // 2, 0, i % 2))
    return pl.pallas_call(
        functools.partial(project_kernel, first, count),
        grid=(4,),
        in_specs=([] if first else [columns])
        + [pl.BlockSpec((512, 512), lambda i: (0, 0))] * (2 * count)
        + [pl.BlockSpec((count, 2, 1, 512, 256), lambda i: (piece // count, 0, i // 2, 0, i % 2))],
        out_specs=columns,
        scratch_shapes=[pltpu.VMEM((512, 1024 * count), BF16)],
        out_shape=jax.ShapeDtypeStruct((2, 512, 512), BF16 if last else F32),
        compiler_params=pltpu.CompilerParams(vmem_limit_bytes=VMEM),
        cost_estimate=COST,
        name="project",
    )(*([] if first else [sums]), *rows, split)


def attend_kernel(length_ref, query_ref, grad_ref, pair_ref, query_out, grads_out, turned_out):
    position = lax.broadcasted_iota(jnp.int32, (512, 1), 0)
    mask = jnp.where(position < length_ref[0], 1.0, 0.0)
    queries, keys, values = [], [], []
    for head in range(2):
        cols = slice(head * HD, (head + 1) * HD)
        query = query_ref[:, cols] * BF16(0.125)
        grad = grad_ref[:, cols]
        key = pair_ref[0, :, cols]
        value = pair_ref[1, :, cols]
        weights = jnp.exp(dot(key, query, NT)) * mask
        attention = weights * (1.0 / jnp.sum(weights, axis=0, keepdims=True))
        low = attention.astype(BF16)
        prob = dot(value, grad, NT)
        row_dot = jnp.sum(low.astype(F32) * prob, axis=0, keepdims=True)
        score = (attention * (prob - row_dot)).astype(BF16)
        queries.append((dot(score, key, TN) * 0.125).astype(BF16))
        keys.append(dot(score, query, NN).astype(BF16))
        values.append(dot(low, grad, NN).astype(BF16))
    query_out[...] = jnp.concatenate(queries, axis=1)
    key_grad = jnp.concatenate(keys, axis=1)
    value_grad = jnp.concatenate(values, axis=1)
    grads_out[0] = key_grad
    grads_out[1] = value_grad
    turned_out[0] = key_grad.T
    turned_out[1] = value_grad.T


def attend(lengths, queries, out_grad, pair):
    block = pl.BlockSpec((512, 128), lambda i, c: (0, i))
    both = pl.BlockSpec((2, 512, 128), lambda i, c: (0, 0, i))
    return pl.pallas_call(
        attend_kernel,
        grid_spec=pltpu.PrefetchScalarGridSpec(
            num_scalar_prefetch=1,
            grid=(4,),
            in_specs=[block, block, both],
            out_specs=[block, both, pl.BlockSpec((2, 128, 512), lambda i, c: (0, i, 0))],
        ),
        out_shape=[
            jax.ShapeDtypeStruct((512, 512), BF16),
            jax.ShapeDtypeStruct((2, 512, 512), BF16),
            jax.ShapeDtypeStruct((2, 512, 512), BF16),
        ],
        compiler_params=pltpu.CompilerParams(vmem_limit_bytes=VMEM),
        cost_estimate=COST,
        name="attend",
    )(lengths, queries, out_grad, pair)


def other_kernel(weight_ref, turned_ref, out_ref):
    total = dot(weight_ref[0, 0, 0], turned_ref[0], NN) + dot(weight_ref[0, 0, 1], turned_ref[1], NN)
    out_ref[0] = total.astype(BF16)


def own_kernel(weight_ref, turned_ref, sent_ref, *outs):
    total = dot(weight_ref[0, 0, 0], turned_ref[0], NN) + dot(weight_ref[0, 0, 1], turned_ref[1], NN)
    total = (total + sent_ref[0].astype(F32)).astype(BF16)
    for i, out_ref in enumerate(outs):

        @pl.when(pl.program_id(0) == i)
        def _():
            out_ref[...] = total


def memory_pieces(split, turned, upper, sent=None):
    rows = pl.BlockSpec((1, 512, 512), lambda i: (i, 0, 0))
    half = 1 if sent is None else 0
    one = jax.ShapeDtypeStruct((512, 512), BF16)
    return pl.pallas_call(
        other_kernel if sent is None else own_kernel,
        grid=(2,),
        in_specs=[
            pl.BlockSpec((1, 1, 2, 512, 512), lambda i: (upper - i, half, 0, 0, 0)),
            pl.BlockSpec((2, 512, 512), lambda i: (0, 0, 0)),
        ]
        + ([] if sent is None else [rows]),
        out_specs=rows if sent is None else [pl.BlockSpec((512, 512), lambda i: (0, 0))] * 2,
        out_shape=jax.ShapeDtypeStruct((2, 512, 512), BF16) if sent is None else [one, one],
        compiler_params=pltpu.CompilerParams(vmem_limit_bytes=VMEM),
        cost_estimate=COST,
        name="memory_pieces",
    )(split, turned, *([] if sent is None else [sent]))


def sum_kernel(at_ref, mine, other, behind, ahead, swapped, g0, g1, g2, out_ref):
    own = pl.program_id(0) < 2
    pairs = ((mine[0], other[0]), (behind[0], swapped[1, 0]), (ahead[0], swapped[0, 0]))
    rows = [jnp.where(own, here, there) for here, there in pairs]
    for kind in range(2):
        out_ref[0, kind] = sum(dot(a, b[kind], NN) for a, b in zip(rows, (g0, g1, g2)))


def last_kernel(at_ref, across, swapped, grads, sums, out_ref):
    rows = jnp.where(pl.program_id(0) < 2, across[0], swapped[0, 0])
    for_key = sums[0, 0] + dot(rows, grads[0], NN)
    for_value = sums[0, 1] + dot(rows, grads[1], NN)
    both = jnp.stack([for_key.astype(BF16), for_value.astype(BF16)], axis=0)
    both = jnp.swapaxes(both, 0, 1).reshape(2, 2, 64, 2, 512)
    out_ref[...] = jnp.swapaxes(both, 0, 1).reshape(2, 1, 2, 1, 64, 2, 512)


HALF = pl.BlockSpec((1, 256, 512), lambda i, at: (i % 2, 0, 0))
SUMS = pl.BlockSpec((1, 2, 256, 512), lambda i, at: (i, 0, 0, 0))


def whole(shape):
    return pl.BlockSpec(shape, lambda i, at: (0,) * len(shape))


def weight_sums(at, mine, other, behind, ahead, swapped, grads):
    return pl.pallas_call(
        sum_kernel,
        grid_spec=pltpu.PrefetchScalarGridSpec(
            num_scalar_prefetch=1,
            grid=(4,),
            in_specs=[HALF] * 4
            + [pl.BlockSpec((2, 1, 256, 512), lambda i, at: (0, i % 2, 0, 0))]
            + [whole((2, 512, 512))] * 3,
            out_specs=SUMS,
        ),
        out_shape=jax.ShapeDtypeStruct((4, 2, 256, 512), F32),
        compiler_params=pltpu.CompilerParams(vmem_limit_bytes=VMEM),
        cost_estimate=COST,
        name="weight_sums",
    )(at, mine, other, behind, ahead, swapped, *grads)


def weight_rows(at, across, swapped, grads, sums):
    out = pl.pallas_call(
        last_kernel,
        grid_spec=pltpu.PrefetchScalarGridSpec(
            num_scalar_prefetch=1,
            grid=(4,),
            in_specs=[HALF, pl.BlockSpec((1, 1, 256, 512), lambda i, at: (2, i % 2, 0, 0))]
            + [whole((2, 512, 512)), SUMS],
            out_specs=pl.BlockSpec(
                (2, 1, 2, 1, 64, 2, 512), lambda i, at: (0, at[1] ^ (i % 2), 0, at[2] ^ (i // 2), 0, 0, 0)
            ),
        ),
        out_shape=jax.ShapeDtypeStruct((2, 2, 2, 2, 64, 2, 512), BF16),
        compiler_params=pltpu.CompilerParams(vmem_limit_bytes=VMEM),
        cost_estimate=COST,
        name="weight_rows",
    )(at, across, swapped, grads, sums)
    return out.reshape(1, 1024, 2, 512)


def body(memory, queries, out_grad, memory_weight, lengths):
    section, tp = lax.axis_index("section"), lax.axis_index("tp")
    dp = lax.axis_index("dp").astype(jnp.int32)
    at = jnp.stack([section // 8, section % 2, tp % 2]).astype(jnp.int32)

    split = split_weights(at, memory_weight[0])
    own = spread(memory[:, 0, :].T, FAR).reshape(512, 512)
    own, split = lax.optimization_barrier((own, split))
    own_other = swap(own)
    from_z, from_x, from_diagonal = near(own, 0, 1), near(own, 1, 0), near(own, 1, 1)
    sums = project(None, [own, own_other], split, 0, False)
    sums, from_z, from_x, from_diagonal = lax.optimization_barrier((sums, from_z, from_x, from_diagonal))
    mine = [own, from_z, from_x, from_diagonal]
    other = [own_other] + [swap(piece) for piece in mine[1:]]
    sums = project(sums, [mine[1], other[1]], split, 1, False)
    pair = project(sums, [mine[2], other[2], mine[3], other[3]], split, 2, True)

    def block_of(pieces, d):
        moved = (d // 2) ^ at[0]
        rows = []
        for dz in range(2):
            piece = jnp.where(moved == 0, pieces[dz], pieces[2 + dz]).reshape(2, 2, 128, 512)
            rows.append(lax.dynamic_slice(piece, (0, d % 2, 0, 0), (2, 1, 128, 512)).reshape(256, 512))
        return jnp.stack(rows)

    way = 1 - 2 * at[2]
    arrived = [along_dp(block_of(mine, (dp + 4 + way * step) % 4), step) for step in (1, -1, 2)]

    query_grad, grads, turned = attend(lengths, queries[0, 0], out_grad[0, 0], pair)
    behind, ahead, across = arrived

    from_behind = along_dp(grads, 1)
    from_ahead = along_dp(grads, -1)
    for_other = memory_pieces(split, turned, 3)
    for_other, behind, ahead, across = lax.optimization_barrier((for_other, behind, ahead, across))
    sent_far = swap(for_other)
    sent_near = swap(memory_pieces(split, turned, 1))
    diagonal, far_x = memory_pieces(split, turned, 3, sent_far)
    from_diagonal, from_x = near(diagonal, 1, 1), near(far_x, 1, 0)
    close_z, close = memory_pieces(split, turned, 1, sent_near)
    from_z = near(close_z, 0, 1)
    terms = (close, from_z, from_x, from_diagonal)
    quarter = sum(term.astype(F32) for term in terms).astype(BF16)
    _, from_behind, from_ahead = lax.optimization_barrier((quarter, from_behind, from_ahead))
    from_across = along_dp(from_behind, 1)
    parts = collect(quarter.reshape(8, 64, 512), FAR)

    swapped = swap(jnp.stack([behind, ahead, across]))
    rows, rows_other = block_of(mine, dp), block_of(other, dp)
    sums = weight_sums(at, rows, rows_other, behind, ahead, swapped, (grads, from_behind, from_ahead))
    sums, from_across = lax.optimization_barrier((sums, from_across))
    weight_grad = weight_rows(at, across, swapped, from_across, sums)
    parts, weight_grad = lax.optimization_barrier((parts, weight_grad))
    memory_grad = jnp.sum(parts.astype(F32), axis=0).astype(BF16).T[:, None, :]
    return memory_grad, query_grad[None, None], weight_grad


def solution(mesh):
    return jax.shard_map(
        body,
        mesh=mesh,
        in_specs=(
            P(None, "dp", ("section", "tp")),
            P("section", "dp", None, "tp"),
            P("section", "dp", None, "tp"),
            P("section", None, None, "tp"),
            P("dp"),
        ),
        out_specs=(
            P(None, "dp", ("section", "tp")),
            P("section", "dp", None, "tp"),
            P("section", "dp", None, "tp"),
        ),
        check_vma=False,
    )
```

```python
import functools

import jax
import jax.numpy as jnp
from jax import lax
from jax.experimental import pallas as pl
from jax.experimental.pallas import tpu as pltpu
from jax.sharding import PartitionSpec as P

PLANE = ("section", "tp")
HD = 64
HEADS = 8
F32 = jnp.float32
COST = pl.CostEstimate(flops=0, bytes_accessed=1 << 16, transcendentals=0)
BF16 = jnp.bfloat16
VMEM = 28 << 20


def index_of(x, z, core):
    x, z = x % 4, z % 8
    return ((x % 2) * 8 + z) * 4 + (x // 2) * 2 + core


def place(i):
    section, tp = divmod(i, 4)
    return (tp // 2) * 2 + section // 8, section % 8, tp % 2


FAR = [
    [index_of(2 * a + px, 2 * b + pz, core) for a in range(2) for b in range(4)]
    for px in range(2)
    for pz in range(2)
    for core in range(2)
]


def beside(value, core):
    return ((value - core) ^ 1) + core


def moves(dx, dz, dcore):
    pairs = []
    for i in range(64):
        x, z, core = place(i)
        pairs.append((i, index_of(beside(x, core) if dx else x, beside(z, core) if dz else z, core ^ dcore)))
    return pairs


NEAR = {(dx, dz): moves(dx, dz, 0) for dx, dz in ((0, 1), (1, 0), (1, 1))}
SWAP = moves(0, 0, 1)


def spread(block, groups):
    count = len(groups[0])
    copies = jnp.broadcast_to(block[None], (count,) + block.shape)
    return lax.all_to_all(copies, PLANE, 0, 0, axis_index_groups=groups)


def collect(blocks, groups):
    return lax.all_to_all(blocks, PLANE, 0, 0, axis_index_groups=groups)


def along_dp(block, step):
    pairs = []
    for tp in range(4):
        for d in range(4):
            pairs.append((tp * 4 + d, tp * 4 + (d + (-step if tp % 2 else step)) % 4))
    return lax.ppermute(block, ("tp", "dp"), pairs)


def swap(block):
    return lax.ppermute(block, PLANE, SWAP)


def near(block, dx, dz):
    return lax.ppermute(block, PLANE, NEAR[dx, dz])


def dot(a, b, dims):
    return lax.dot_general(a, b, (dims, ((), ())), preferred_element_type=F32)


NN = ((1,), (0,))
NT = ((1,), (1,))
TN = ((0,), (0,))


def split_kernel(at_ref, weight_ref, out_ref):
    weight = weight_ref[...].reshape(4, 2, 64, 2, 512)
    weight = jnp.swapaxes(weight, 0, 1).reshape(512, 2, 512)
    out_ref[...] = jnp.swapaxes(weight, 0, 1).reshape(1, 1, 2, 512, 512)


def split_weights(at, weight):
    view = weight.reshape(2, 4, 2, 2, 2, 64, 2, 512)
    return pl.pallas_call(
        split_kernel,
        grid_spec=pltpu.PrefetchScalarGridSpec(
            num_scalar_prefetch=1,
            grid=(4, 2),
            in_specs=[
                pl.BlockSpec(
                    (1, 4, 1, 2, 1, 64, 2, 512),
                    lambda r, h, at: (at[0] ^ (r // 2), 0, at[1] ^ (r % 2), 0, at[2] ^ h, 0, 0, 0),
                )
            ],
            out_specs=pl.BlockSpec((1, 1, 2, 512, 512), lambda r, h, at: (r, h, 0, 0, 0)),
        ),
        out_shape=jax.ShapeDtypeStruct((4, 2, 2, 512, 512), BF16),
        compiler_params=pltpu.CompilerParams(vmem_limit_bytes=VMEM),
        cost_estimate=COST,
        name="split_weights",
    )(at, view)


def project_kernel(first, count, *refs):
    sums_ref = None if first else refs[0]
    rows_refs = refs[0 if first else 1 :][: 2 * count]
    weight_ref, out_ref, turned = refs[-3:]

    @pl.when(pl.program_id(0) == 0)
    def _():
        for i, rows in enumerate(rows_refs):
            turned[:, i * 512 : (i + 1) * 512] = rows[...].T

    weight = weight_ref[...].reshape(count * 1024, 256)
    total = dot(turned[...], weight, NN)
    if not first:
        total += sums_ref[0]
    out_ref[0] = total.astype(out_ref.dtype)


def project(sums, rows, split, piece, last):
    first, count = sums is None, len(rows) // 2
    columns = pl.BlockSpec((1, 512, 256), lambda i: (i // 2, 0, i % 2))
    return pl.pallas_call(
        functools.partial(project_kernel, first, count),
        grid=(4,),
        in_specs=([] if first else [columns])
        + [pl.BlockSpec((512, 512), lambda i: (0, 0))] * (2 * count)
        + [pl.BlockSpec((count, 2, 1, 512, 256), lambda i: (piece // count, 0, i // 2, 0, i % 2))],
        out_specs=columns,
        scratch_shapes=[pltpu.VMEM((512, 1024 * count), BF16)],
        out_shape=jax.ShapeDtypeStruct((2, 512, 512), BF16 if last else F32),
        compiler_params=pltpu.CompilerParams(vmem_limit_bytes=VMEM),
        cost_estimate=COST,
        name="project",
    )(*([] if first else [sums]), *rows, split)


def attend_kernel(length_ref, query_ref, grad_ref, pair_ref, query_out, grads_out, turned_out):
    position = lax.broadcasted_iota(jnp.int32, (512, 1), 0)
    mask = jnp.where(position < length_ref[0], 1.0, 0.0)
    queries, keys, values = [], [], []
    for head in range(2):
        cols = slice(head * HD, (head + 1) * HD)
        query = query_ref[:, cols] * BF16(0.125)
        grad = grad_ref[:, cols]
        key = pair_ref[0, :, cols]
        value = pair_ref[1, :, cols]
        weights = jnp.exp(dot(key, query, NT)) * mask
        attention = weights * (1.0 / jnp.sum(weights, axis=0, keepdims=True))
        low = attention.astype(BF16)
        prob = dot(value, grad, NT)
        row_dot = jnp.sum(low.astype(F32) * prob, axis=0, keepdims=True)
        score = (attention * (prob - row_dot)).astype(BF16)
        queries.append((dot(score, key, TN) * 0.125).astype(BF16))
        keys.append(dot(score, query, NN).astype(BF16))
        values.append(dot(low, grad, NN).astype(BF16))
    query_out[...] = jnp.concatenate(queries, axis=1)
    key_grad = jnp.concatenate(keys, axis=1)
    value_grad = jnp.concatenate(values, axis=1)
    grads_out[0] = key_grad
    grads_out[1] = value_grad
    turned_out[0] = key_grad.T
    turned_out[1] = value_grad.T


def attend(lengths, queries, out_grad, pair):
    block = pl.BlockSpec((512, 128), lambda i, c: (0, i))
    both = pl.BlockSpec((2, 512, 128), lambda i, c: (0, 0, i))
    return pl.pallas_call(
        attend_kernel,
        grid_spec=pltpu.PrefetchScalarGridSpec(
            num_scalar_prefetch=1,
            grid=(4,),
            in_specs=[block, block, both],
            out_specs=[block, both, pl.BlockSpec((2, 128, 512), lambda i, c: (0, i, 0))],
        ),
        out_shape=[
            jax.ShapeDtypeStruct((512, 512), BF16),
            jax.ShapeDtypeStruct((2, 512, 512), BF16),
            jax.ShapeDtypeStruct((2, 512, 512), BF16),
        ],
        compiler_params=pltpu.CompilerParams(vmem_limit_bytes=VMEM),
        cost_estimate=COST,
        name="attend",
    )(lengths, queries, out_grad, pair)


def other_kernel(weight_ref, turned_ref, out_ref):
    total = dot(weight_ref[0, 0, 0], turned_ref[0], NN) + dot(weight_ref[0, 0, 1], turned_ref[1], NN)
    out_ref[0] = total.astype(BF16)


def own_kernel(weight_ref, turned_ref, sent_ref, *outs):
    total = dot(weight_ref[0, 0, 0], turned_ref[0], NN) + dot(weight_ref[0, 0, 1], turned_ref[1], NN)
    total = (total + sent_ref[0].astype(F32)).astype(BF16)
    for i, out_ref in enumerate(outs):

        @pl.when(pl.program_id(0) == i)
        def _():
            out_ref[...] = total


def memory_pieces(split, turned, upper, sent=None):
    rows = pl.BlockSpec((1, 512, 512), lambda i: (i, 0, 0))
    half = 1 if sent is None else 0
    one = jax.ShapeDtypeStruct((512, 512), BF16)
    return pl.pallas_call(
        other_kernel if sent is None else own_kernel,
        grid=(2,),
        in_specs=[
            pl.BlockSpec((1, 1, 2, 512, 512), lambda i: (upper - i, half, 0, 0, 0)),
            pl.BlockSpec((2, 512, 512), lambda i: (0, 0, 0)),
        ]
        + ([] if sent is None else [rows]),
        out_specs=rows if sent is None else [pl.BlockSpec((512, 512), lambda i: (0, 0))] * 2,
        out_shape=jax.ShapeDtypeStruct((2, 512, 512), BF16) if sent is None else [one, one],
        compiler_params=pltpu.CompilerParams(vmem_limit_bytes=VMEM),
        cost_estimate=COST,
        name="memory_pieces",
    )(split, turned, *([] if sent is None else [sent]))


def sum_kernel(at_ref, mine, other, behind, ahead, swapped, g0, g1, g2, out_ref):
    own = pl.program_id(0) < 2
    pairs = ((mine[0], other[0]), (behind[0], swapped[1, 0]), (ahead[0], swapped[0, 0]))
    rows = [jnp.where(own, here, there) for here, there in pairs]
    for kind in range(2):
        out_ref[0, kind] = sum(dot(a, b[kind], NN) for a, b in zip(rows, (g0, g1, g2)))


def last_kernel(at_ref, across, swapped, grads, sums, out_ref):
    rows = jnp.where(pl.program_id(0) < 2, across[0], swapped[0, 0])
    for_key = sums[0, 0] + dot(rows, grads[0], NN)
    for_value = sums[0, 1] + dot(rows, grads[1], NN)
    both = jnp.stack([for_key.astype(BF16), for_value.astype(BF16)], axis=0)
    both = jnp.swapaxes(both, 0, 1).reshape(2, 2, 64, 2, 512)
    out_ref[...] = jnp.swapaxes(both, 0, 1).reshape(2, 1, 2, 1, 64, 2, 512)


HALF = pl.BlockSpec((1, 256, 512), lambda i, at: (i % 2, 0, 0))
SUMS = pl.BlockSpec((1, 2, 256, 512), lambda i, at: (i, 0, 0, 0))


def whole(shape):
    return pl.BlockSpec(shape, lambda i, at: (0,) * len(shape))


def weight_sums(at, mine, other, behind, ahead, swapped, grads):
    return pl.pallas_call(
        sum_kernel,
        grid_spec=pltpu.PrefetchScalarGridSpec(
            num_scalar_prefetch=1,
            grid=(4,),
            in_specs=[HALF] * 4
            + [pl.BlockSpec((2, 1, 256, 512), lambda i, at: (0, i % 2, 0, 0))]
            + [whole((2, 512, 512))] * 3,
            out_specs=SUMS,
        ),
        out_shape=jax.ShapeDtypeStruct((4, 2, 256, 512), F32),
        compiler_params=pltpu.CompilerParams(vmem_limit_bytes=VMEM),
        cost_estimate=COST,
        name="weight_sums",
    )(at, mine, other, behind, ahead, swapped, *grads)


def weight_rows(at, across, swapped, grads, sums):
    out = pl.pallas_call(
        last_kernel,
        grid_spec=pltpu.PrefetchScalarGridSpec(
            num_scalar_prefetch=1,
            grid=(4,),
            in_specs=[HALF, pl.BlockSpec((1, 1, 256, 512), lambda i, at: (2, i % 2, 0, 0))]
            + [whole((2, 512, 512)), SUMS],
            out_specs=pl.BlockSpec(
                (2, 1, 2, 1, 64, 2, 512), lambda i, at: (0, at[1] ^ (i % 2), 0, at[2] ^ (i // 2), 0, 0, 0)
            ),
        ),
        out_shape=jax.ShapeDtypeStruct((2, 2, 2, 2, 64, 2, 512), BF16),
        compiler_params=pltpu.CompilerParams(vmem_limit_bytes=VMEM),
        cost_estimate=pl.CostEstimate(flops=1 << 30, bytes_accessed=12 << 20, transcendentals=0),
        name="weight_rows",
    )(at, across, swapped, grads, sums)
    return out.reshape(1, 1024, 2, 512)


def body(memory, queries, out_grad, memory_weight, lengths):
    section, tp = lax.axis_index("section"), lax.axis_index("tp")
    dp = lax.axis_index("dp").astype(jnp.int32)
    at = jnp.stack([section // 8, section % 2, tp % 2]).astype(jnp.int32)

    split = split_weights(at, memory_weight[0])
    own = spread(memory[:, 0, :].T, FAR).reshape(512, 512)
    own, split = lax.optimization_barrier((own, split))
    own_other = swap(own)
    from_z, from_x, from_diagonal = near(own, 0, 1), near(own, 1, 0), near(own, 1, 1)
    sums = project(None, [own, own_other], split, 0, False)
    sums, from_z, from_x, from_diagonal = lax.optimization_barrier((sums, from_z, from_x, from_diagonal))
    mine = [own, from_z, from_x, from_diagonal]
    other = [own_other] + [swap(piece) for piece in mine[1:]]
    sums = project(sums, [mine[1], other[1]], split, 1, False)
    pair = project(sums, [mine[2], other[2], mine[3], other[3]], split, 2, True)

    def block_of(pieces, d):
        moved = (d // 2) ^ at[0]
        rows = []
        for dz in range(2):
            piece = jnp.where(moved == 0, pieces[dz], pieces[2 + dz]).reshape(2, 2, 128, 512)
            rows.append(lax.dynamic_slice(piece, (0, d % 2, 0, 0), (2, 1, 128, 512)).reshape(256, 512))
        return jnp.stack(rows)

    way = 1 - 2 * at[2]
    arrived = [along_dp(block_of(mine, (dp + 4 + way * step) % 4), step) for step in (1, -1, 2)]

    query_grad, grads, turned = attend(lengths, queries[0, 0], out_grad[0, 0], pair)
    behind, ahead, across = arrived
    grads, turned, behind, ahead = lax.optimization_barrier((grads, turned, behind, ahead))

    from_behind = along_dp(grads, 1)
    from_ahead = along_dp(grads, -1)
    for_other, across = lax.optimization_barrier((memory_pieces(split, turned, 3), across))
    sent_far = swap(for_other)
    sent_near = swap(memory_pieces(split, turned, 1))
    diagonal, far_x = memory_pieces(split, turned, 3, sent_far)
    from_diagonal, from_x = near(diagonal, 1, 1), near(far_x, 1, 0)
    close_z, close = memory_pieces(split, turned, 1, sent_near)
    from_z = near(close_z, 0, 1)
    terms = (close, from_z, from_x, from_diagonal)
    quarter = sum(term.astype(F32) for term in terms).astype(BF16)
    _, from_behind, from_ahead = lax.optimization_barrier((quarter, from_behind, from_ahead))
    from_across = along_dp(from_behind, 1)
    parts = collect(quarter.reshape(8, 64, 512), FAR)

    swapped = swap(jnp.stack([behind, ahead, across]))
    rows, rows_other = block_of(mine, dp), block_of(other, dp)
    sums = weight_sums(at, rows, rows_other, behind, ahead, swapped, (grads, from_behind, from_ahead))
    sums, from_across = lax.optimization_barrier((sums, from_across))
    weight_grad = weight_rows(at, across, swapped, from_across, sums)
    parts, weight_grad = lax.optimization_barrier((parts, weight_grad))
    memory_grad = jnp.sum(parts.astype(F32), axis=0).astype(BF16).T[:, None, :]
    return memory_grad, query_grad[None, None], weight_grad


def solution(mesh):
    return jax.shard_map(
        body,
        mesh=mesh,
        in_specs=(
            P(None, "dp", ("section", "tp")),
            P("section", "dp", None, "tp"),
            P("section", "dp", None, "tp"),
            P("section", None, None, "tp"),
            P("dp"),
        ),
        out_specs=(
            P(None, "dp", ("section", "tp")),
            P("section", "dp", None, "tp"),
            P("section", "dp", None, "tp"),
        ),
        check_vma=False,
    )
```
